256 devices in a mesh: leaf: 128 (over x, z, y), top: 2 (over core).
Axes of the slice: x: 4, y: 4, z: 8, core: 2. Of those that a mesh axis runs over, the one named last changes fastest.
Arguments:
- leaf_multipoles: bfloat16 [121, 32768], P(None, ('leaf', 'top')), may hold values from -6 to 6
- upward_ops: bfloat16 [121, 968], replicated, may hold values from -0.1875 to 0.1875
- transfer_ops: bfloat16 [121, 38236], replicated, may hold values from -0.046875 to 0.046875
- downward_ops: bfloat16 [121, 968], replicated, may hold values from -0.5 to 0.5
- send_lists: int32 [256, 128, 16], P(('leaf', 'top')), may hold values from 0 to 128, as said below
- leaf_pairs: int32 [316, 32768], P(None, 'leaf'), may hold values from 0 to 4352, as said below
- top_pairs: int32 [316, 4096], P(None, 'leaf'), may hold values from 0 to 4096, as said below
Outputs:
- leaf_locals: float32 [121, 32768], P(None, ('leaf', 'top'))
The draws below stay inside these ranges and needn't reach their ends.
Inputs may be any that keep to these rules, and one draw needn't show every extreme that they name: send_lists[b, i, s] is a leaf cell of block b, counted within the block; 128 marks an unused slot. Used slots come before unused ones, cells in one list are distinct, and a block sends nothing to its own chip. leaf_pairs[c, t] is a column of the source table of the chip holding t, or 4352 where class c has no source; columns of unused received slots never appear. top_pairs[c, q] is a coarse cell, or 4096 where class c has no source.
All inputs are finite; a program needn't handle non-finite values.
Results may differ from the reference program's by a relative error of at most 0.0029.
Values may be sent and summed in bfloat16 or wider, within the bound.
No kernel may reach another device: no remote copies, remote signals or barrier semaphores. Data moves between devices by JAX's collectives and lax.ppermute only.
A program may use at most 128 MiB of HBM per device.

```python
import jax
import jax.numpy as jnp
from jax import lax

NCOEF = 121
CLASSES = 316
CELLS = 128
SLOTS = 16
TOPD = 16
LEAF_TOTAL = 32768
TOP_TOTAL = 4096
TABLE = 4352
N_LEAF = 128
N_TOP = 2


def grid_place(index):
    places = [jnp.zeros_like(index), jnp.zeros_like(index), jnp.zeros_like(index)]
    for bit_number in range(18):
        bit_value = jnp.bitwise_and(jnp.right_shift(index, bit_number), 1)
        places[bit_number % 3] = places[bit_number % 3] + jnp.left_shift(bit_value, bit_number // 3)
    return places


def send_table(key):
    blocks = N_LEAF * N_TOP
    near_key = jax.random.fold_in(key, 1)
    cell_key = jax.random.fold_in(key, 2)
    chip_index = jnp.arange(blocks, dtype=jnp.int32)[:, None] // N_TOP
    peer_index = jnp.arange(N_LEAF, dtype=jnp.int32)[None, :]
    chip_place = grid_place(chip_index)
    peer_place = grid_place(peer_index)
    reach = jnp.maximum(jnp.maximum(jnp.abs(chip_place[0] - peer_place[0]), jnp.abs(chip_place[1] - peer_place[1])), jnp.abs(chip_place[2] - peer_place[2]))
    is_near = (reach <= 1) & (peer_index != chip_index)
    near_fill = jax.random.randint(near_key, (blocks, N_LEAF), SLOTS // 2, SLOTS + 1)
    slot_fill = jnp.where(is_near, near_fill, 0)
    full_peer = (chip_index + N_LEAF // 2) % N_LEAF
    slot_fill = jnp.where(peer_index == full_peer, SLOTS, slot_fill)
    perm_keys = jax.random.split(cell_key, blocks * N_LEAF)
    chosen_cells = jax.vmap(lambda subkey: jax.random.permutation(subkey, CELLS)[:SLOTS])(perm_keys)
    chosen_cells = chosen_cells.reshape(blocks, N_LEAF, SLOTS)
    is_live = jnp.arange(SLOTS, dtype=jnp.int32)[None, None, :] < slot_fill[:, :, None]
    return jnp.where(is_live, chosen_cells, CELLS).astype(jnp.int32)


def draw_send_lists(key, part):
    return send_table(key)


def draw_leaf_pairs(key, part):
    sends = send_table(key)
    key = jax.random.fold_in(key, 11)
    live_key, side_key, local_key, remote_key = jax.random.split(key, 4)
    usable = sends < CELLS
    usable = usable.reshape(N_LEAF, N_TOP, N_LEAF, SLOTS).transpose(2, 1, 0, 3).reshape(N_LEAF, N_TOP * N_LEAF * SLOTS)
    prefix_count = jnp.cumsum(usable.astype(jnp.int32), axis=1)
    usable_count = prefix_count[:, -1]
    draw_shape = (N_LEAF, CLASSES, N_TOP * CELLS)
    chosen_rank = jax.random.randint(remote_key, draw_shape, 0, usable_count[:, None, None])
    found_slot = jax.vmap(lambda ranks, prefix: jnp.searchsorted(prefix, ranks.reshape(-1), side='right'))(chosen_rank, prefix_count)
    remote_slot = N_TOP * CELLS + found_slot.reshape(draw_shape).astype(jnp.int32)
    local_slot = jax.random.randint(local_key, draw_shape, 0, N_TOP * CELLS)
    far_side = jax.random.randint(side_key, draw_shape, 0, 2)
    source_slot = jnp.where(far_side == 1, remote_slot, local_slot)
    is_live = jax.random.randint(live_key, draw_shape, 0, 5) < 3
    result_list = jnp.where(is_live, source_slot, TABLE)
    return result_list.transpose(1, 0, 2).reshape(CLASSES, LEAF_TOTAL).astype(jnp.int32)


def draw_top_pairs(key, part):
    key = jax.random.fold_in(key, 23)
    live_key, source_key = jax.random.split(key, 2)
    draw_shape = (CLASSES, TOP_TOTAL)
    source_cell = jax.random.randint(source_key, draw_shape, 0, TOP_TOTAL)
    is_live = jax.random.randint(live_key, draw_shape, 0, 5) < 3
    return jnp.where(is_live, source_cell, TOP_TOTAL).astype(jnp.int32)


def level_of(key, shape, pieces, least, largest):
    factor_of = 1.0
    for position, parts in pieces:
        draws = jax.random.uniform(jax.random.fold_in(jax.random.fold_in(key, 6), position), (parts,), jnp.float32, least / len(pieces), largest / len(pieces))
        factor_of = factor_of * jnp.repeat(jnp.exp(draws), shape[position] // parts).reshape((-1,) + (1,) * (len(shape) - 1 - position))
    return factor_of


def gaussian(own_key, extent, deviation, most, shards=(), kind=jnp.bfloat16):
    gain = level_of(own_key, extent, shards, -0.22, 0.18) if shards else 1.0
    values = jax.random.normal(own_key, extent, jnp.float32) * deviation * gain
    return jnp.minimum(jnp.maximum(values, -most), most).astype(kind)


def setup_inputs(seed: int = 0) -> dict:
    key_of = jax.random.split(jax.random.key(seed), 8)
    return {
        "leaf_multipoles": gaussian(key_of[0], (NCOEF, LEAF_TOTAL), 1.0, 6.0, ((1, 256),)),
        "upward_ops": gaussian(key_of[1], (NCOEF, 8 * NCOEF), (8 * NCOEF) ** -0.5, 0.1875),
        "transfer_ops": gaussian(key_of[2], (NCOEF, CLASSES * NCOEF), (NCOEF * CLASSES // 2) ** -0.5, 0.046875),
        "downward_ops": gaussian(key_of[3], (NCOEF, 8 * NCOEF), NCOEF ** -0.5, 0.5),
        "send_lists": draw_send_lists(jax.random.fold_in(key_of[7], 71), 0),
        "leaf_pairs": draw_leaf_pairs(jax.random.fold_in(key_of[7], 71), 0),
        "top_pairs": draw_top_pairs(jax.random.fold_in(key_of[7], 71), 0),
    }


class_groups = 4


def with_zero(source_table):
    return jnp.concatenate([source_table, jnp.zeros((source_table.shape[0], 1), source_table.dtype)], axis=1)


def translate(source_table, pair_lists, operators):
    order_terms = source_table.shape[0]
    per_group = pair_lists.shape[0] // class_groups
    summed = jnp.zeros((order_terms, pair_lists.shape[1]), jnp.float32)
    for group_index in range(class_groups):
        first_class = group_index * per_group
        picked = jnp.take(source_table, pair_lists[first_class:first_class + per_group], axis=1)
        operator_block = operators[:, first_class * order_terms:(first_class + per_group) * order_terms]
        operator_block = operator_block.reshape(order_terms, per_group, order_terms)
        summed = summed + jnp.einsum("ico,ict->ot", operator_block.astype(jnp.float32), picked.astype(jnp.float32))
    return summed


def reference(leaf_multipoles, upward_ops, transfer_ops, downward_ops, send_lists, leaf_pairs, top_pairs):
    children = leaf_multipoles.reshape(NCOEF, TOP_TOTAL, 8).astype(jnp.float32)
    upward = upward_ops.reshape(NCOEF, 8, NCOEF).astype(jnp.float32)
    coarse_multi = jnp.einsum("iko,iqk->oq", upward, children).astype(jnp.bfloat16)
    coarse_table = with_zero(coarse_multi)
    chip_pairs = top_pairs.reshape(CLASSES, N_LEAF, N_TOP * TOPD).transpose(1, 0, 2)
    coarse_local = lax.map(lambda pairs_here: translate(coarse_table, pairs_here, transfer_ops), chip_pairs)
    coarse_local = coarse_local.transpose(1, 0, 2).reshape(NCOEF, TOP_TOTAL).astype(jnp.bfloat16)
    downward = downward_ops.reshape(NCOEF, 8, NCOEF).astype(jnp.float32)
    from_coarse = jnp.einsum("iko,iq->oqk", downward, coarse_local.astype(jnp.float32)).reshape(NCOEF, LEAF_TOTAL)
    padded = with_zero(leaf_multipoles)
    block_start = (jnp.arange(N_LEAF * N_TOP, dtype=jnp.int32) * CELLS)[:, None, None]
    columns = jnp.where(send_lists < CELLS, send_lists + block_start, LEAF_TOTAL).astype(jnp.int32)
    columns = columns.reshape(N_LEAF, N_TOP, N_LEAF, SLOTS).transpose(2, 1, 0, 3).reshape(N_LEAF, N_TOP * N_LEAF * SLOTS)
    near_pairs = leaf_pairs.reshape(CLASSES, N_LEAF, N_TOP * CELLS).transpose(1, 0, 2)

    def chip_pass(inputs):
        chip_index, chip_columns, chip_lists = inputs
        own_cells = lax.dynamic_slice_in_dim(leaf_multipoles, chip_index * (N_TOP * CELLS), N_TOP * CELLS, 1)
        source_table = with_zero(jnp.concatenate([own_cells, jnp.take(padded, chip_columns, axis=1)], axis=1))
        return translate(source_table, chip_lists, transfer_ops)

    near_local = lax.map(chip_pass, (jnp.arange(N_LEAF, dtype=jnp.int32), columns, near_pairs))
    near_local = near_local.transpose(1, 0, 2).reshape(NCOEF, LEAF_TOTAL)
    return near_local + from_coarse
```

```python
import functools

import jax
import jax.numpy as jnp
from jax import lax
from jax.experimental import pallas as pl
from jax.experimental.pallas import tpu as pltpu
from jax.sharding import PartitionSpec as P

BF = jnp.bfloat16
F32 = jnp.float32
I32 = jnp.int32

WIDTH = 128
GROUP = 8
TILE = 512
HALF = TILE // 2
BLOCK = 128


def nt_dot(left, right):
    return lax.dot_general(
        left, right, (((1,), (1,)), ((), ())), preferred_element_type=F32
    )


def dot(left, right):
    return jnp.dot(left, right, preferred_element_type=F32)


def main_kernel(
    flag_lane,
    core_ref,
    coarse_pos,
    arrived,
    local_cells,
    pairs,
    operators,
    downward,
    keep,
    send,
    places,
    tables,
    coarse_rows,
    picked,
    near_sum,
    coarse_sum,
):
    core = core_ref[0]
    peers, rows_each, width = arrived.shape
    slots = rows_each // 2
    slot_count = peers * slots
    class_count, targets = pairs.shape
    groups = places.shape[0] // GROUP
    coarse_targets = coarse_sum.shape[1]
    local_count = local_cells.shape[1]

    received = arrived[:, :slots, :].reshape(slot_count, width)
    flag_pick = (lax.broadcasted_iota(I32, (16, width), 1) == flag_lane).astype(F32).astype(BF)
    flags = nt_dot(flag_pick, received)
    by_peer = (
        lax.broadcasted_iota(I32, (slot_count, peers), 0) // slots
        == lax.broadcasted_iota(I32, (slot_count, peers), 1)
    )
    counts = dot(flags.astype(BF), by_peer.astype(F32).astype(BF))
    before = (
        lax.broadcasted_iota(I32, (peers, peers), 0) < lax.broadcasted_iota(I32, (peers, peers), 1)
    )
    first = dot(counts.astype(BF), before.astype(F32).astype(BF))[:8].astype(I32) + local_count
    used = jnp.sum(counts[0:1, :]).astype(I32)
    tile_count = (local_count + used + TILE - 1) // TILE

    lane = lax.broadcasted_iota(I32, (8, peers), 1)
    dest_parts = []
    for part in range(slots):
        slot = lane + part * peers
        at = jnp.take_along_axis(first, slot // slots, axis=1) + slot % slots
        live = flags[:8, part * peers : (part + 1) * peers] > 0.5
        dest_parts.append(jnp.where(live, at, -1))
    dest = jnp.concatenate(dest_parts, axis=1)[0:1]

    def place(row, _):
        start = pl.multiple_of(row * 8, 8)
        inside = pairs[pl.ds(start, 8), :]
        places[pl.ds(start, 8), :] = place_rows(inside)
        return 0

    def place_rows(column):
        parts = []
        for half in range(targets // peers):
            col = column[:, half * peers : (half + 1) * peers]
            slot = col - 2 * local_count - core * slot_count
            mine = (slot >= 0) & (slot < slot_count)
            safe = jnp.where(mine, slot, 0)
            far = jnp.take_along_axis(first, safe // slots, axis=1) + safe % slots
            near = col - core * local_count
            parts.append(
                jnp.where(mine, far, jnp.where((near >= 0) & (near < local_count), near, -1))
            )
        return jnp.concatenate(parts, axis=1)

    whole = class_count // 8
    lax.fori_loop(0, whole, place, 0)
    tail = class_count - whole * 8
    if tail:
        rest = pairs[whole * 8 : class_count, :]
        rest = jnp.concatenate([rest, jnp.full((8 - tail, targets), 1 << 20, I32)], axis=0)
        places[whole * 8 : whole * 8 + 8, :] = place_rows(rest)

    def pack(tile, _):
        for part in range(TILE // peers):
            base = tile * TILE + part * peers
            one_hot = (
                lax.broadcasted_iota(I32, (peers, slot_count), 0) + base == dest
            ).astype(F32).astype(BF)
            cells = dot(one_hot, received).T.astype(BF)
            half, at = divmod(part * peers, HALF)
            tables[tile, half * width : (half + 1) * width, at : at + peers] = cells
        return 0

    lax.fori_loop(0, tile_count, pack, 0)
    tables[0, :width, :local_count] = local_cells[...]

    coarse_rows[:slot_count, :] = arrived[:, slots:, :].reshape(slot_count, width).astype(F32)
    coarse_rows[slot_count:, :] = jnp.zeros((8, width), F32)

    near_sum[...] = jnp.zeros_like(near_sum)
    coarse_sum[...] = jnp.zeros_like(coarse_sum)
    row_index = lax.broadcasted_iota(I32, (HALF, targets), 0)

    def gather(table, position):
        inside = (position >= 0) & (position < TILE)
        low = jnp.where(inside, position & (HALF - 1), -1)
        one_hot = jnp.where(row_index == low, 1.0, 0.0).astype(BF)
        both = dot(table, one_hot)
        return jnp.where(position >= HALF, both[width:], both[:width]).astype(BF)

    def near_step(table, group, base):
        position = places[pl.ds(pl.multiple_of(group * GROUP, GROUP), GROUP), :] - base
        total = near_sum[...]
        for pair in range(GROUP // 2):
            cells = jnp.concatenate(
                [gather(table, position[2 * pair + j : 2 * pair + j + 1]) for j in range(2)], axis=0
            )
            total = total + dot(operator_pair(group, pair), cells)
        near_sum[...] = total

    def operator_pair(group, pair):
        start = pl.multiple_of((group * GROUP + 2 * pair) * width, 2 * width)
        return operators[:, pl.ds(start, 2 * width)]

    def first_tile(group, _):
        base = group * (GROUP * coarse_targets)
        for row in range(GROUP * coarse_targets):
            picked[pl.ds(row, 1), :] = coarse_rows[pl.ds(coarse_pos[base + row], 1), :]
        near_step(tables[0], group, 0)
        total = coarse_sum[...]
        for pair in range(GROUP // 2):
            at = 2 * pair * coarse_targets
            cells = jnp.concatenate(
                [
                    picked[at + j * coarse_targets : at + (j + 1) * coarse_targets, :].astype(BF)
                    for j in range(2)
                ],
                axis=1,
            )
            total = total + nt_dot(operator_pair(group, pair), cells)
        coarse_sum[...] = total
        return 0

    lax.fori_loop(0, groups, first_tile, 0)

    def more_tiles(tile, _):
        table = tables[tile]

        def step(group, _):
            near_step(table, group, tile * TILE)
            return 0

        return lax.fori_loop(0, groups, step, 0)

    lax.fori_loop(1, tile_count, more_tiles, 0)

    children = targets // coarse_targets
    spread = (
        lax.broadcasted_iota(I32, (coarse_targets, targets), 1) // children
        == lax.broadcasted_iota(I32, (coarse_targets, targets), 0)
    ).astype(F32).astype(BF)
    child = lax.broadcasted_iota(I32, (width, targets), 1) % children
    total = near_sum[...]
    real = lax.broadcasted_iota(I32, (width, coarse_targets), 0) < flag_lane
    rest = jnp.where(real, coarse_sum[...], 0.0)
    for _ in range(2):
        term = rest.astype(BF)
        rest = rest - term.astype(F32)
        wide = dot(term, spread)
        stacked = jnp.concatenate(
            [jnp.where(child == k, wide, 0.0).astype(BF) for k in range(children)], axis=0
        )
        total = total + dot(downward[...], stacked)
    left, right = total[:, :local_count], total[:, local_count:]
    keep[...] = jnp.where(core == 0, left, right)
    send[...] = jnp.where(core == 0, right, left)


def arrange(operators, order_terms):
    class_count = operators.shape[1] // order_terms
    arranged = operators.reshape(order_terms, class_count, order_terms).transpose(2, 1, 0)
    pad = WIDTH - order_terms
    arranged = jnp.pad(arranged, ((0, pad), (0, 0), (0, pad)))
    return arranged.reshape(WIDTH, class_count * WIDTH)


def arrange_kernel(class_count, source, arranged, rows):
    lines, order_terms = source.shape
    step = pl.program_id(0)
    rows[:, order_terms:] = jnp.zeros((lines + 8, WIDTH - order_terms), F32)
    rows[lines:, :] = jnp.zeros((8, WIDTH), F32)

    def widen(block, _):
        start = pl.multiple_of(block * WIDTH, WIDTH)
        rows[pl.ds(start, WIDTH), :order_terms] = source[pl.ds(start, WIDTH), :].astype(F32)
        return 0

    lax.fori_loop(0, lines // WIDTH, widen, 0, unroll=4)

    def cut(index, _):
        start = pl.multiple_of(index * WIDTH, WIDTH)
        real = step * BLOCK + index < class_count
        square = jnp.where(real, rows[pl.ds(index * order_terms, WIDTH), :], 0.0)
        arranged[:, pl.ds(start, WIDTH)] = square.astype(BF)
        return 0

    lax.fori_loop(0, BLOCK, cut, 0, unroll=4)


def arrange_classes(operators, order_terms):
    class_count = operators.shape[0] // order_terms
    padded_count = (class_count + GROUP - 1) // GROUP * GROUP
    lines = BLOCK * order_terms
    steps = (class_count + BLOCK - 1) // BLOCK
    return pl.pallas_call(
        functools.partial(arrange_kernel, class_count),
        grid=(steps,),
        out_shape=jax.ShapeDtypeStruct((WIDTH, padded_count * WIDTH), BF),
        in_specs=[pl.BlockSpec((lines, order_terms), lambda step: (step, 0))],
        out_specs=pl.BlockSpec((WIDTH, BLOCK * WIDTH), lambda step: (0, step)),
        scratch_shapes=[pltpu.VMEM((lines + 8, WIDTH), F32)],
        compiler_params=pltpu.CompilerParams(vmem_limit_bytes=40 << 20),
        cost_estimate=pl.CostEstimate(
            flops=0, bytes_accessed=40 * 1024 * 1024, transcendentals=0
        ),
    )(operators)


def outgoing_kernel(cells, chosen, upward, outgoing, spread, risen):
    order_terms, cell_count = cells.shape
    slots, peers = chosen.shape
    coarse_count = cell_count // 8
    pad = WIDTH - order_terms
    values = cells[...].astype(F32)
    flag = (lax.broadcasted_iota(I32, (pad, cell_count), 0) == 0).astype(F32)
    flagged = jnp.concatenate([values, flag], axis=0).astype(BF)
    columns = jnp.concatenate(
        [chosen[...].astype(F32), jnp.zeros((peers - slots, peers), F32)], axis=0
    ).T.astype(I32)
    cell = lax.broadcasted_iota(I32, (peers, cell_count), 1)
    for slot in range(slots):
        one_hot = (cell == columns[:, slot : slot + 1]).astype(F32).astype(BF)
        spread[pl.ds(slot, peers, stride=slots), :] = nt_dot(one_hot, flagged)
    outgoing[:, :slots, :] = spread[...].astype(BF).reshape(peers, slots, WIDTH)

    risen[: 8 * order_terms, :] = dot(upward[...], cells[...])
    risen[8 * order_terms :, :] = jnp.zeros((8, cell_count), F32)
    child = lax.broadcasted_iota(I32, (WIDTH, cell_count), 1) % 8
    total = jnp.zeros((WIDTH, cell_count), F32)
    for k in range(8):
        total = total + jnp.where(child == k, risen[pl.ds(k * order_terms, WIDTH), :], 0.0)
    real = lax.broadcasted_iota(I32, (WIDTH, cell_count), 0) < order_terms
    total = jnp.where(real, total, 0.0).T
    coarse = jnp.sum(total.reshape(coarse_count, 8, WIDTH), axis=1).astype(BF)
    outgoing[:, slots:, :] = jnp.broadcast_to(coarse[None], (peers, coarse_count, WIDTH))


def per_device(
    leaf_multipoles, upward_ops, transfer_ops, downward_ops, send_lists, leaf_pairs, top_pairs
):
    order_terms, cell_count = leaf_multipoles.shape
    _, peers, slots = send_lists.shape
    class_count, targets = leaf_pairs.shape
    coarse_targets = top_pairs.shape[1]
    coarse_count = cell_count // 8
    core = lax.axis_index("top").astype(I32)
    vmem = pl.BlockSpec(memory_space=pltpu.VMEM)
    smem = pl.BlockSpec(memory_space=pltpu.SMEM)

    outgoing = pl.pallas_call(
        outgoing_kernel,
        out_shape=jax.ShapeDtypeStruct((peers, slots + coarse_count, WIDTH), BF),
        in_specs=[vmem] * 3,
        out_specs=vmem,
        scratch_shapes=[
            pltpu.VMEM((peers * slots, WIDTH), F32),
            pltpu.VMEM((8 * order_terms + 8, cell_count), F32),
        ],
        compiler_params=pltpu.CompilerParams(vmem_limit_bytes=16 << 20),
    )(leaf_multipoles, send_lists[0].T, upward_ops.T)
    arrived = lax.all_to_all(outgoing, "leaf", split_axis=0, concat_axis=0, tiled=True)

    local_cells = jnp.pad(leaf_multipoles, ((0, WIDTH - order_terms), (0, 0)))
    operators = arrange_classes(transfer_ops.T, order_terms)
    downward = arrange(downward_ops, order_terms)
    padded_classes = operators.shape[1] // WIDTH
    source_core = (top_pairs // coarse_count) % 2
    source_row = top_pairs // (2 * coarse_count) * coarse_count + top_pairs % coarse_count
    zero_row = peers * coarse_count
    held = (source_core == core) & (top_pairs < 2 * zero_row)
    coarse_pos = jnp.where(held, source_row, zero_row)
    coarse_pos = jnp.pad(
        coarse_pos, ((0, padded_classes - class_count), (0, 0)), constant_values=zero_row
    ).reshape(-1)

    most_tiles = (cell_count + peers * slots + TILE - 1) // TILE
    half_shape = jax.ShapeDtypeStruct((WIDTH, cell_count), F32)
    keep, send = pl.pallas_call(
        functools.partial(main_kernel, order_terms),
        out_shape=(half_shape, half_shape),
        in_specs=[smem, smem] + [vmem] * 5,
        out_specs=(vmem, vmem),
        scratch_shapes=[
            pltpu.VMEM((padded_classes, targets), I32),
            pltpu.VMEM((most_tiles, 2 * WIDTH, HALF), BF),
            pltpu.VMEM((zero_row + 8, WIDTH), F32),
            pltpu.VMEM((GROUP * coarse_targets, WIDTH), F32),
            pltpu.VMEM((WIDTH, targets), F32),
            pltpu.VMEM((WIDTH, coarse_targets), F32),
        ],
        compiler_params=pltpu.CompilerParams(vmem_limit_bytes=40 << 20),
    )(core.reshape(1), coarse_pos, arrived, local_cells, leaf_pairs, operators, downward)
    other = lax.ppermute(send, "top", [(0, 1), (1, 0)])
    return (keep + other)[:order_terms]


def solution(mesh):
    in_specs = (
        P(None, ("leaf", "top")),
        P(),
        P(),
        P(),
        P(("leaf", "top"), None, None),
        P(None, "leaf"),
        P(None, "leaf"),
    )
    out_specs = P(None, ("leaf", "top"))
    return jax.shard_map(
        per_device, mesh=mesh, in_specs=in_specs, out_specs=out_specs, check_vma=False
    )
```

```python
import functools

import jax
import jax.numpy as jnp
from jax import lax
from jax.experimental import pallas as pl
from jax.experimental.pallas import tpu as pltpu
from jax.sharding import PartitionSpec as P

BF = jnp.bfloat16
F32 = jnp.float32
I32 = jnp.int32

WIDTH = 128
GROUP = 8
TILE = 512
HALF = TILE // 2
BY_PRODUCT = (0, 3, 6)
BLOCK = 128


def nt_dot(left, right):
    return lax.dot_general(
        left, right, (((1,), (1,)), ((), ())), preferred_element_type=F32
    )


def dot(left, right):
    return jnp.dot(left, right, preferred_element_type=F32)


def main_kernel(
    flag_lane,
    core_ref,
    coarse_pos,
    arrived,
    local_cells,
    pairs,
    stored_operators,
    downward,
    keep,
    send,
    operators,
    arrival,
    places,
    tables,
    columns,
    coarse_rows,
    picked,
    cells,
    near_sum,
    coarse_sum,
):
    fetch = pltpu.make_async_copy(stored_operators, operators, arrival)
    fetch.start()
    core = core_ref[0]
    peers, rows_each, width = arrived.shape
    slots = rows_each // 2
    slot_count = peers * slots
    class_count, targets = pairs.shape
    groups = places.shape[0] // GROUP
    coarse_targets = coarse_sum.shape[1]
    local_count = local_cells.shape[1]

    received = arrived[:, :slots, :].reshape(slot_count, width)
    flag_pick = (lax.broadcasted_iota(I32, (16, width), 1) == flag_lane).astype(F32).astype(BF)
    flags = nt_dot(flag_pick, received)
    by_peer = (
        lax.broadcasted_iota(I32, (slot_count, peers), 0) // slots
        == lax.broadcasted_iota(I32, (slot_count, peers), 1)
    )
    counts = dot(flags.astype(BF), by_peer.astype(F32).astype(BF))
    before = (
        lax.broadcasted_iota(I32, (peers, peers), 0) < lax.broadcasted_iota(I32, (peers, peers), 1)
    )
    first = dot(counts.astype(BF), before.astype(F32).astype(BF))[:8].astype(I32) + local_count
    used = jnp.sum(counts[0:1, :]).astype(I32)
    tile_count = (local_count + used + TILE - 1) // TILE

    lane = lax.broadcasted_iota(I32, (8, peers), 1)
    dest_parts = []
    for part in range(slots):
        slot = lane + part * peers
        at = jnp.take_along_axis(first, slot // slots, axis=1) + slot % slots
        live = flags[:8, part * peers : (part + 1) * peers] > 0.5
        dest_parts.append(jnp.where(live, at, -1))
    dest = jnp.concatenate(dest_parts, axis=1)[0:1]

    def place(row, _):
        start = pl.multiple_of(row * 8, 8)
        inside = pairs[pl.ds(start, 8), :]
        places[pl.ds(start, 8), :] = place_rows(inside)
        return 0

    def place_rows(column):
        parts = []
        for half in range(targets // peers):
            col = column[:, half * peers : (half + 1) * peers]
            slot = col - 2 * local_count - core * slot_count
            mine = (slot >= 0) & (slot < slot_count)
            safe = jnp.where(mine, slot, 0)
            far = jnp.take_along_axis(first, safe // slots, axis=1) + safe % slots
            near = col - core * local_count
            parts.append(
                jnp.where(mine, far, jnp.where((near >= 0) & (near < local_count), near, -1))
            )
        return jnp.concatenate(parts, axis=1)

    whole = class_count // 8
    lax.fori_loop(0, whole, place, 0, unroll=4)
    tail = class_count - whole * 8
    if tail:
        rest = pairs[whole * 8 : class_count, :]
        rest = jnp.concatenate([rest, jnp.full((8 - tail, targets), 1 << 20, I32)], axis=0)
        places[whole * 8 : whole * 8 + 8, :] = place_rows(rest)

    def pack(tile, _):
        for part in range(TILE // peers):
            base = tile * TILE + part * peers
            one_hot = (
                lax.broadcasted_iota(I32, (peers, slot_count), 0) + base == dest
            ).astype(F32).astype(BF)
            packed = dot(one_hot, received).T.astype(BF)
            half, at = divmod(part * peers, HALF)
            tables[tile, half * width : (half + 1) * width, at : at + peers] = packed
            columns[tile, part] = packed.astype(F32)
        return 0

    lax.fori_loop(0, tile_count, pack, 0)
    tables[0, :width, :local_count] = local_cells[...]
    columns[0, 0] = local_cells[...].astype(F32)

    coarse_rows[:slot_count, :] = arrived[:, slots:, :].reshape(slot_count, width).astype(F32)
    coarse_rows[slot_count:, :] = jnp.zeros((8, width), F32)

    near_sum[...] = jnp.zeros_like(near_sum)
    coarse_sum[...] = jnp.zeros_like(coarse_sum)
    row_index = lax.broadcasted_iota(I32, (HALF, targets), 0)

    def gather(table, position):
        inside = (position >= 0) & (position < TILE)
        low = jnp.where(inside, position & (HALF - 1), -1)
        one_hot = jnp.where(row_index == low, 1.0, 0.0).astype(BF)
        both = dot(table, one_hot)
        return jnp.where(position >= HALF, both[width:], both[:width]).astype(BF)

    def lane_gather(tile, position):
        blocks = []
        for half in range(targets // width):
            at = position[:, half * width : (half + 1) * width]
            lane_at = jnp.broadcast_to(at & (width - 1), (8, width))
            block = jnp.broadcast_to(at // width, (8, width))
            block = jnp.where(jnp.broadcast_to(at, (8, width)) < 0, -1, block)
            lines = []
            for line in range(0, width, 8):
                found = jnp.zeros((8, width), F32)
                for part in range(TILE // width):
                    picked_cells = jnp.take_along_axis(
                        columns[tile, part, line : line + 8, :], lane_at, axis=1
                    )
                    found = jnp.where(block == part, picked_cells, found)
                lines.append(found)
            blocks.append(jnp.concatenate(lines, axis=0))
        return jnp.concatenate(blocks, axis=1).astype(BF)

    def operator_pair(group, pair):
        start = pl.multiple_of((group * GROUP + 2 * pair) * width, 2 * width)
        return operators[:, pl.ds(start, 2 * width)]

    def near_step(table, tile, group, base, gather_now=True):
        if gather_now:
            position = places[pl.ds(pl.multiple_of(group * GROUP, GROUP), GROUP), :] - base
        total = near_sum[...]
        for pair in range(GROUP // 2):
            here = slice(2 * pair * width, 2 * (pair + 1) * width)
            ready = jnp.maximum(group - 1, 0)
            total = total + dot(operator_pair(ready, pair), cells[here, :])
            if gather_now:
                for c in (2 * pair, 2 * pair + 1):
                    row = position[c : c + 1]
                    cells[c * width : (c + 1) * width, :] = (
                        gather(table, row) if c in BY_PRODUCT else lane_gather(tile, row)
                    )
        near_sum[...] = total

    def coarse_step(group, gather_now=True):
        total = coarse_sum[...]
        ready = jnp.maximum(group - 1, 0)
        base = group * (GROUP * coarse_targets)
        for pair in range(GROUP // 2):
            at = 2 * pair * coarse_targets
            both = jnp.concatenate(
                [
                    picked[at + j * coarse_targets : at + (j + 1) * coarse_targets, :].astype(BF)
                    for j in range(2)
                ],
                axis=1,
            )
            total = total + nt_dot(operator_pair(ready, pair), both)
            if gather_now:
                for row in range(at, at + 2 * coarse_targets):
                    picked[pl.ds(row, 1), :] = coarse_rows[pl.ds(coarse_pos[base + row], 1), :]
        coarse_sum[...] = total

    picked[...] = jnp.zeros_like(picked)
    cells[...] = jnp.zeros_like(cells)

    def first_tile(group, _):
        near_step(tables[0], 0, group, 0)
        coarse_step(group)
        return 0

    fetch.wait()
    lax.fori_loop(0, groups, first_tile, 0)
    coarse_step(groups, False)
    near_step(None, 0, groups, 0, False)

    def more_tiles(tile, _):
        table = tables[tile]
        cells[...] = jnp.zeros_like(cells)

        def step(group, _):
            near_step(table, tile, group, tile * TILE)
            return 0

        lax.fori_loop(0, groups, step, 0)
        near_step(None, tile, groups, 0, False)
        return 0

    lax.fori_loop(1, tile_count, more_tiles, 0)

    children = targets // coarse_targets
    spread = (
        lax.broadcasted_iota(I32, (coarse_targets, targets), 1) // children
        == lax.broadcasted_iota(I32, (coarse_targets, targets), 0)
    ).astype(F32).astype(BF)
    child = lax.broadcasted_iota(I32, (width, targets), 1) % children
    total = near_sum[...]
    real = lax.broadcasted_iota(I32, (width, coarse_targets), 0) < flag_lane
    rest = jnp.where(real, coarse_sum[...], 0.0)
    for _ in range(2):
        term = rest.astype(BF)
        rest = rest - term.astype(F32)
        wide = dot(term, spread)
        stacked = jnp.concatenate(
            [jnp.where(child == k, wide, 0.0).astype(BF) for k in range(children)], axis=0
        )
        total = total + dot(downward[...], stacked)
    left, right = total[:, :local_count], total[:, local_count:]
    keep[...] = jnp.where(core == 0, left, right)
    send[...] = jnp.where(core == 0, right, left)


def arrange(operators, order_terms):
    class_count = operators.shape[1] // order_terms
    arranged = operators.reshape(order_terms, class_count, order_terms).transpose(2, 1, 0)
    pad = WIDTH - order_terms
    arranged = jnp.pad(arranged, ((0, pad), (0, 0), (0, pad)))
    return arranged.reshape(WIDTH, class_count * WIDTH)


def arrange_kernel(class_count, source, arranged, rows):
    lines, order_terms = source.shape
    step = pl.program_id(0)
    rows[:, order_terms:] = jnp.zeros((lines + 8, WIDTH - order_terms), F32)
    rows[lines:, :] = jnp.zeros((8, WIDTH), F32)

    def widen(block, _):
        start = pl.multiple_of(block * WIDTH, WIDTH)
        rows[pl.ds(start, WIDTH), :order_terms] = source[pl.ds(start, WIDTH), :].astype(F32)
        return 0

    lax.fori_loop(0, lines // WIDTH, widen, 0, unroll=4)

    def cut(index, _):
        start = pl.multiple_of(index * WIDTH, WIDTH)
        real = step * BLOCK + index < class_count
        square = jnp.where(real, rows[pl.ds(index * order_terms, WIDTH), :], 0.0)
        arranged[:, pl.ds(start, WIDTH)] = square.astype(BF)
        return 0

    lax.fori_loop(0, BLOCK, cut, 0, unroll=4)


def arrange_classes(operators, order_terms):
    class_count = operators.shape[0] // order_terms
    padded_count = (class_count + GROUP - 1) // GROUP * GROUP
    lines = BLOCK * order_terms
    steps = (class_count + BLOCK - 1) // BLOCK
    return pl.pallas_call(
        functools.partial(arrange_kernel, class_count),
        grid=(steps,),
        out_shape=jax.ShapeDtypeStruct((WIDTH, padded_count * WIDTH), BF),
        in_specs=[pl.BlockSpec((lines, order_terms), lambda step: (step, 0))],
        out_specs=pl.BlockSpec((WIDTH, BLOCK * WIDTH), lambda step: (0, step)),
        scratch_shapes=[pltpu.VMEM((lines + 8, WIDTH), F32)],
        compiler_params=pltpu.CompilerParams(vmem_limit_bytes=40 << 20),
        cost_estimate=pl.CostEstimate(
            flops=0, bytes_accessed=40 * 1024 * 1024, transcendentals=0
        ),
    )(operators)


def outgoing_kernel(cells, chosen, upward, outgoing, spread, risen):
    order_terms, cell_count = cells.shape
    slots, peers = chosen.shape
    coarse_count = cell_count // 8
    pad = WIDTH - order_terms
    values = cells[...].astype(F32)
    flag = (lax.broadcasted_iota(I32, (pad, cell_count), 0) == 0).astype(F32)
    flagged = jnp.concatenate([values, flag], axis=0).astype(BF)
    columns = jnp.concatenate(
        [chosen[...].astype(F32), jnp.zeros((peers - slots, peers), F32)], axis=0
    ).T.astype(I32)
    cell = lax.broadcasted_iota(I32, (peers, cell_count), 1)
    for slot in range(slots):
        one_hot = (cell == columns[:, slot : slot + 1]).astype(F32).astype(BF)
        spread[pl.ds(slot, peers, stride=slots), :] = nt_dot(one_hot, flagged)
    outgoing[:, :slots, :] = spread[...].astype(BF).reshape(peers, slots, WIDTH)

    risen[: 8 * order_terms, :] = dot(upward[...], cells[...])
    risen[8 * order_terms :, :] = jnp.zeros((8, cell_count), F32)
    child = lax.broadcasted_iota(I32, (WIDTH, cell_count), 1) % 8
    total = jnp.zeros((WIDTH, cell_count), F32)
    for k in range(8):
        total = total + jnp.where(child == k, risen[pl.ds(k * order_terms, WIDTH), :], 0.0)
    real = lax.broadcasted_iota(I32, (WIDTH, cell_count), 0) < order_terms
    total = jnp.where(real, total, 0.0).T
    coarse = jnp.sum(total.reshape(coarse_count, 8, WIDTH), axis=1).astype(BF)
    outgoing[:, slots:, :] = jnp.broadcast_to(coarse[None], (peers, coarse_count, WIDTH))


def per_device(
    leaf_multipoles, upward_ops, transfer_ops, downward_ops, send_lists, leaf_pairs, top_pairs
):
    order_terms, cell_count = leaf_multipoles.shape
    _, peers, slots = send_lists.shape
    class_count, targets = leaf_pairs.shape
    coarse_targets = top_pairs.shape[1]
    coarse_count = cell_count // 8
    core = lax.axis_index("top").astype(I32)
    vmem = pl.BlockSpec(memory_space=pltpu.VMEM)
    smem = pl.BlockSpec(memory_space=pltpu.SMEM)

    outgoing = pl.pallas_call(
        outgoing_kernel,
        out_shape=jax.ShapeDtypeStruct((peers, slots + coarse_count, WIDTH), BF),
        in_specs=[vmem] * 3,
        out_specs=vmem,
        scratch_shapes=[
            pltpu.VMEM((peers * slots, WIDTH), F32),
            pltpu.VMEM((8 * order_terms + 8, cell_count), F32),
        ],
        compiler_params=pltpu.CompilerParams(vmem_limit_bytes=16 << 20),
    )(leaf_multipoles, send_lists[0].T, upward_ops.T)
    arrived = lax.all_to_all(outgoing, "leaf", split_axis=0, concat_axis=0, tiled=True)

    local_cells = jnp.pad(leaf_multipoles, ((0, WIDTH - order_terms), (0, 0)))
    operators = arrange_classes(transfer_ops.T, order_terms)
    downward = arrange(downward_ops, order_terms)
    padded_classes = operators.shape[1] // WIDTH
    source_core = (top_pairs // coarse_count) % 2
    source_row = top_pairs // (2 * coarse_count) * coarse_count + top_pairs % coarse_count
    zero_row = peers * coarse_count
    held = (source_core == core) & (top_pairs < 2 * zero_row)
    coarse_pos = jnp.where(held, source_row, zero_row)
    coarse_pos = jnp.pad(
        coarse_pos, ((0, padded_classes - class_count), (0, 0)), constant_values=zero_row
    ).reshape(-1)

    most_tiles = (cell_count + peers * slots + TILE - 1) // TILE
    half_shape = jax.ShapeDtypeStruct((WIDTH, cell_count), F32)
    keep, send = pl.pallas_call(
        functools.partial(main_kernel, order_terms),
        out_shape=(half_shape, half_shape),
        in_specs=[smem, smem] + [vmem] * 3 + [pl.BlockSpec(memory_space=pl.ANY), vmem],
        out_specs=(vmem, vmem),
        scratch_shapes=[
            pltpu.VMEM(operators.shape, BF),
            pltpu.SemaphoreType.DMA,
            pltpu.VMEM((padded_classes, targets), I32),
            pltpu.VMEM((most_tiles, 2 * WIDTH, HALF), BF),
            pltpu.VMEM((most_tiles, TILE // WIDTH, WIDTH, WIDTH), F32),
            pltpu.VMEM((zero_row + 8, WIDTH), F32),
            pltpu.VMEM((GROUP * coarse_targets, WIDTH), F32),
            pltpu.VMEM((GROUP * WIDTH, targets), BF),
            pltpu.VMEM((WIDTH, targets), F32),
            pltpu.VMEM((WIDTH, coarse_targets), F32),
        ],
        compiler_params=pltpu.CompilerParams(vmem_limit_bytes=60 << 20),
    )(core.reshape(1), coarse_pos, arrived, local_cells, leaf_pairs, operators, downward)
    other = lax.ppermute(send, "top", [(0, 1), (1, 0)])
    return (keep + other)[:order_terms]


def solution(mesh):
    in_specs = (
        P(None, ("leaf", "top")),
        P(),
        P(),
        P(),
        P(("leaf", "top"), None, None),
        P(None, "leaf"),
        P(None, "leaf"),
    )
    out_specs = P(None, ("leaf", "top"))
    return jax.shard_map(
        per_device, mesh=mesh, in_specs=in_specs, out_specs=out_specs, check_vma=False
    )
```

```python
import functools

import jax
import jax.numpy as jnp
from jax import lax
from jax.experimental import pallas as pl
from jax.experimental.pallas import tpu as pltpu
from jax.sharding import PartitionSpec as P

BF = jnp.bfloat16
F32 = jnp.float32
I32 = jnp.int32

WIDTH = 128
GROUP = 16
TILE = 384
HALF = 256
FETCHES = 4
SPAN = 8
BY_PRODUCT = (0, 3, 6, 8, 11, 14)
BLOCK = 128


def nt_dot(left, right):
    return lax.dot_general(
        left, right, (((1,), (1,)), ((), ())), preferred_element_type=F32
    )


def dot(left, right):
    return jnp.dot(left, right, preferred_element_type=F32)


def main_kernel(
    flag_lane,
    core_ref,
    coarse_pos,
    arrived,
    pairs,
    local_sum,
    stored_operators,
    downward,
    keep,
    send,
    operators,
    arrivals,
    places,
    tables,
    columns,
    coarse_rows,
    picked,
    cells,
    near_sum,
    coarse_sum,
):
    piece = operators.shape[1] // FETCHES

    def fetch(index):
        span = pl.ds(pl.multiple_of(index * piece, WIDTH), piece)
        return pltpu.make_async_copy(
            stored_operators.at[:, span], operators.at[:, span], arrivals.at[index]
        )

    for index in range(FETCHES):
        fetch(index).start()
    core = core_ref[0]
    peers, rows_each, width = arrived.shape
    slots = rows_each // 2
    slot_count = peers * slots
    class_count, targets = pairs.shape
    groups = places.shape[0] // GROUP
    coarse_targets = coarse_sum.shape[1]
    local_count = targets // 2

    received = arrived[:, :slots, :].reshape(slot_count, width)
    flag_pick = (lax.broadcasted_iota(I32, (16, width), 1) == flag_lane).astype(F32).astype(BF)
    flags = nt_dot(flag_pick, received)
    by_peer = (
        lax.broadcasted_iota(I32, (slot_count, peers), 0) // slots
        == lax.broadcasted_iota(I32, (slot_count, peers), 1)
    )
    counts = dot(flags.astype(BF), by_peer.astype(F32).astype(BF))
    before = (
        lax.broadcasted_iota(I32, (peers, peers), 0) < lax.broadcasted_iota(I32, (peers, peers), 1)
    )
    first = dot(counts.astype(BF), before.astype(F32).astype(BF))[:8].astype(I32)
    used = jnp.sum(counts[0:1, :]).astype(I32)
    tile_count = (used + TILE - 1) // TILE

    lane = lax.broadcasted_iota(I32, (8, peers), 1)
    dest_parts = []
    for part in range(slots):
        slot = lane + part * peers
        at = jnp.take_along_axis(first, slot // slots, axis=1) + slot % slots
        live = flags[:8, part * peers : (part + 1) * peers] > 0.5
        dest_parts.append(jnp.where(live, at, -1))
    dest = jnp.concatenate(dest_parts, axis=1)[0:1]

    def place_rows(column):
        lines = column.shape[0]
        from_peer = jnp.broadcast_to(first[0:1], (lines, peers))
        parts = []
        for half in range(targets // peers):
            col = column[:, half * peers : (half + 1) * peers]
            slot = col - 2 * local_count - core * slot_count
            mine = (slot >= 0) & (slot < slot_count)
            safe = jnp.where(mine, slot, 0)
            far = jnp.take_along_axis(from_peer, safe // slots, axis=1) + safe % slots
            parts.append(jnp.where(mine, far, -1))
        return jnp.concatenate(parts, axis=1)

    lines = 32

    def place(block, _):
        start = pl.multiple_of(block * lines, lines)
        places[pl.ds(start, lines), :] = place_rows(pairs[pl.ds(start, lines), :])
        return 0

    whole = class_count // lines * lines
    lax.fori_loop(0, whole // lines, place, 0)
    for start in range(whole, class_count, 8):
        count = min(8, class_count - start)
        places[start : start + count, :] = place_rows(pairs[start : start + count, :])
    places[class_count:, :] = jnp.full((places.shape[0] - class_count, targets), -1, I32)

    def pack(tile, _):
        for part in range(TILE // peers):
            base = tile * TILE + part * peers
            one_hot = (
                lax.broadcasted_iota(I32, (peers, slot_count), 0) + base == dest
            ).astype(F32).astype(BF)
            packed = dot(one_hot, received).T.astype(BF)
            half, at = divmod(part * peers, HALF)
            tables[tile, half * width : (half + 1) * width, at : at + peers] = packed
            columns[tile, part] = packed.astype(F32)
        return 0

    tables[...] = jnp.zeros_like(tables)
    lax.fori_loop(0, jnp.maximum(tile_count, 1), pack, 0)

    coarse_rows[:slot_count, :] = arrived[:, slots:, :].reshape(slot_count, width).astype(F32)
    coarse_rows[slot_count:, :] = jnp.zeros((8, width), F32)

    near_sum[...] = local_sum[...]
    coarse_sum[...] = jnp.zeros_like(coarse_sum)
    row_index = lax.broadcasted_iota(I32, (HALF, targets), 0)

    def gather(table, position):
        inside = (position >= 0) & (position < TILE)
        low = jnp.where(inside, position & (HALF - 1), -1)
        one_hot = jnp.where(row_index == low, 1.0, 0.0).astype(BF)
        both = dot(table, one_hot)
        return jnp.where(position >= HALF, both[width:], both[:width]).astype(BF)

    def lane_gather(tile, position):
        blocks = []
        for half in range(targets // width):
            at = position[:, half * width : (half + 1) * width]
            lane_at = jnp.broadcast_to(at & (width - 1), (8, width))
            block = jnp.broadcast_to(at // width, (8, width))
            block = jnp.where(jnp.broadcast_to(at, (8, width)) < 0, -1, block)
            lines = []
            for line in range(0, width, 8):
                found = jnp.zeros((8, width), F32)
                for part in range(TILE // width):
                    picked_cells = jnp.take_along_axis(
                        columns[tile, part, line : line + 8, :], lane_at, axis=1
                    )
                    found = jnp.where(block == part, picked_cells, found)
                lines.append(found)
            blocks.append(jnp.concatenate(lines, axis=0))
        return jnp.concatenate(blocks, axis=1).astype(BF)

    def operator_pair(group, pair):
        start = pl.multiple_of((group * GROUP + 2 * pair) * width, 2 * width)
        return operators[:, pl.ds(start, 2 * width)]

    def operator_span(group, pair):
        start = pl.multiple_of((group * GROUP + 2 * pair) * width, 2 * width)
        return operators[:, pl.ds(start, 2 * SPAN * width)]

    def near_step(table, tile, group, base, gather_now=True):
        if gather_now:
            position = places[pl.ds(pl.multiple_of(group * GROUP, GROUP), GROUP), :] - base
        total = near_sum[...]
        for pair in range(GROUP // 2):
            here = slice(2 * pair * width, 2 * (pair + SPAN) * width)
            ready = jnp.maximum(group - 1, 0)
            if pair % SPAN == 0:
                total = total + dot(operator_span(ready, pair), cells[here, :])
            if gather_now:
                for c in (2 * pair, 2 * pair + 1):
                    row = position[c : c + 1]
                    cells[c * width : (c + 1) * width, :] = (
                        gather(table, row) if c in BY_PRODUCT else lane_gather(tile, row)
                    )
        near_sum[...] = total

    def coarse_step(group, gather_now=True):
        total = coarse_sum[...]
        ready = jnp.maximum(group - 1, 0)
        base = group * (GROUP * coarse_targets)
        for pair in range(GROUP // 2):
            at = 2 * pair * coarse_targets
            both = jnp.concatenate(
                [
                    picked[at + j * coarse_targets : at + (j + 1) * coarse_targets, :].astype(BF)
                    for j in range(2)
                ],
                axis=1,
            )
            total = total + nt_dot(operator_pair(ready, pair), both)
            if gather_now:
                for row in range(at, at + 2 * coarse_targets):
                    picked[pl.ds(row, 1), :] = coarse_rows[pl.ds(coarse_pos[base + row], 1), :]
        coarse_sum[...] = total

    picked[...] = jnp.zeros_like(picked)
    cells[...] = jnp.zeros_like(cells)

    def first_tile(group, _):
        near_step(tables[0], 0, group, 0)
        coarse_step(group)
        return 0

    steps = groups // FETCHES

    def fetched(index, _):
        fetch(index).wait()
        return lax.fori_loop(index * steps, (index + 1) * steps, first_tile, 0)

    lax.fori_loop(0, FETCHES, fetched, 0)
    coarse_step(groups, False)
    near_step(None, 0, groups, 0, False)

    def more_tiles(tile, _):
        table = tables[tile]
        cells[...] = jnp.zeros_like(cells)

        def step(group, _):
            near_step(table, tile, group, tile * TILE)
            return 0

        lax.fori_loop(0, groups, step, 0)
        near_step(None, tile, groups, 0, False)
        return 0

    lax.fori_loop(1, tile_count, more_tiles, 0)

    children = targets // coarse_targets
    spread = (
        lax.broadcasted_iota(I32, (coarse_targets, targets), 1) // children
        == lax.broadcasted_iota(I32, (coarse_targets, targets), 0)
    ).astype(F32).astype(BF)
    child = lax.broadcasted_iota(I32, (width, targets), 1) % children
    total = near_sum[...]
    real = lax.broadcasted_iota(I32, (width, coarse_targets), 0) < flag_lane
    rest = jnp.where(real, coarse_sum[...], 0.0)
    for _ in range(2):
        term = rest.astype(BF)
        rest = rest - term.astype(F32)
        wide = dot(term, spread)
        stacked = jnp.concatenate(
            [jnp.where(child == k, wide, 0.0).astype(BF) for k in range(children)], axis=0
        )
        total = total + dot(downward[...], stacked)
    left, right = total[:, :local_count], total[:, local_count:]
    keep[...] = jnp.where(core == 0, left, right)
    send[...] = jnp.where(core == 0, right, left)


def local_kernel(core_ref, local_cells, pairs, operators, local_sum, places, columns, cells):
    width, local_count = local_cells.shape
    class_count, targets = pairs.shape
    groups = places.shape[0] // GROUP
    first = core_ref[0] * local_count
    places[:class_count, :] = pairs[...] - first
    places[class_count:, :] = jnp.full((places.shape[0] - class_count, targets), -1, I32)
    columns[...] = local_cells[...].astype(F32)
    cells[...] = jnp.zeros_like(cells)
    local_sum[...] = jnp.zeros_like(local_sum)

    def translate(group):
        start = pl.multiple_of(group * GROUP * width, GROUP * width)
        local_sum[...] += dot(operators[:, pl.ds(start, GROUP * width)], cells[...])

    def step(group, _):
        translate(jnp.maximum(group - 1, 0))
        position = places[pl.ds(pl.multiple_of(group * GROUP, GROUP), GROUP), :]
        for c in range(GROUP):
            for half in range(targets // width):
                span = slice(half * width, (half + 1) * width)
                at = jnp.broadcast_to(position[c : c + 1, span], (8, width))
                live = (at >= 0) & (at < local_count)
                lane_at = at & (local_count - 1)
                lines = [
                    jnp.where(
                        live,
                        jnp.take_along_axis(columns[line : line + 8, :], lane_at, axis=1),
                        0.0,
                    )
                    for line in range(0, width, 8)
                ]
                cells[c * width : (c + 1) * width, span] = jnp.concatenate(lines, axis=0).astype(BF)
        return 0

    lax.fori_loop(0, groups, step, 0)
    translate(groups - 1)


def arrange(operators, order_terms):
    class_count = operators.shape[1] // order_terms
    arranged = operators.reshape(order_terms, class_count, order_terms).transpose(2, 1, 0)
    pad = WIDTH - order_terms
    arranged = jnp.pad(arranged, ((0, pad), (0, 0), (0, pad)))
    return arranged.reshape(WIDTH, class_count * WIDTH)


def arrange_kernel(class_count, source, arranged, rows):
    lines, order_terms = source.shape
    whole = rows.shape[0] - 8
    rows[:, order_terms:] = jnp.zeros((whole + 8, WIDTH - order_terms), F32)
    rows[whole:, :] = jnp.zeros((8, WIDTH), F32)
    for done in range(0, class_count, BLOCK):
        here = min(BLOCK, class_count - done)
        count = here * order_terms
        start = done * order_terms

        def widen(block, _):
            at = pl.multiple_of(block * WIDTH, WIDTH)
            rows[pl.ds(at, WIDTH), :order_terms] = source[pl.ds(start + at, WIDTH), :].astype(F32)
            return 0

        lax.fori_loop(0, count // WIDTH, widen, 0, unroll=4)
        left = count % WIDTH
        if left:
            rows[count - left : count, :order_terms] = source[
                start + count - left : start + count, :
            ].astype(F32)

        def cut(index, _):
            at = pl.multiple_of((done + index) * WIDTH, WIDTH)
            arranged[:, pl.ds(at, WIDTH)] = rows[pl.ds(index * order_terms, WIDTH), :].astype(BF)
            return 0

        lax.fori_loop(0, here, cut, 0, unroll=4)
    spare = arranged.shape[1] - class_count * WIDTH
    arranged[:, class_count * WIDTH :] = jnp.zeros((WIDTH, spare), BF)


def arrange_classes(operators, order_terms):
    class_count = operators.shape[0] // order_terms
    padded_count = (class_count + GROUP - 1) // GROUP * GROUP
    vmem = pl.BlockSpec(memory_space=pltpu.VMEM)
    return pl.pallas_call(
        functools.partial(arrange_kernel, class_count),
        out_shape=jax.ShapeDtypeStruct((WIDTH, padded_count * WIDTH), BF),
        in_specs=[vmem],
        out_specs=vmem,
        scratch_shapes=[pltpu.VMEM((BLOCK * order_terms + 8, WIDTH), F32)],
        compiler_params=pltpu.CompilerParams(vmem_limit_bytes=32 << 20),
        cost_estimate=pl.CostEstimate(
            flops=0, bytes_accessed=40 * 1024 * 1024, transcendentals=0
        ),
    )(operators)


def outgoing_kernel(cells, chosen, upward, outgoing, spread, risen):
    order_terms, cell_count = cells.shape
    slots, peers = chosen.shape
    coarse_count = cell_count // 8
    pad = WIDTH - order_terms
    values = cells[...].astype(F32)
    flag = (lax.broadcasted_iota(I32, (pad, cell_count), 0) == 0).astype(F32)
    flagged = jnp.concatenate([values, flag], axis=0).astype(BF)
    columns = jnp.concatenate(
        [chosen[...].astype(F32), jnp.zeros((peers - slots, peers), F32)], axis=0
    ).T.astype(I32)
    cell = lax.broadcasted_iota(I32, (peers, cell_count), 1)
    for slot in range(slots):
        one_hot = (cell == columns[:, slot : slot + 1]).astype(F32).astype(BF)
        spread[pl.ds(slot, peers, stride=slots), :] = nt_dot(one_hot, flagged)
    outgoing[:, :slots, :] = spread[...].astype(BF).reshape(peers, slots, WIDTH)

    risen[: 8 * order_terms, :] = dot(upward[...], cells[...])
    risen[8 * order_terms :, :] = jnp.zeros((8, cell_count), F32)
    child = lax.broadcasted_iota(I32, (WIDTH, cell_count), 1) % 8
    total = jnp.zeros((WIDTH, cell_count), F32)
    for k in range(8):
        total = total + jnp.where(child == k, risen[pl.ds(k * order_terms, WIDTH), :], 0.0)
    real = lax.broadcasted_iota(I32, (WIDTH, cell_count), 0) < order_terms
    total = jnp.where(real, total, 0.0).T
    coarse = jnp.sum(total.reshape(coarse_count, 8, WIDTH), axis=1).astype(BF)
    outgoing[:, slots:, :] = jnp.broadcast_to(coarse[None], (peers, coarse_count, WIDTH))


def per_device(
    leaf_multipoles, upward_ops, transfer_ops, downward_ops, send_lists, leaf_pairs, top_pairs
):
    order_terms, cell_count = leaf_multipoles.shape
    _, peers, slots = send_lists.shape
    class_count, targets = leaf_pairs.shape
    coarse_targets = top_pairs.shape[1]
    coarse_count = cell_count // 8
    core = lax.axis_index("top").astype(I32)
    vmem = pl.BlockSpec(memory_space=pltpu.VMEM)
    smem = pl.BlockSpec(memory_space=pltpu.SMEM)

    outgoing = pl.pallas_call(
        outgoing_kernel,
        out_shape=jax.ShapeDtypeStruct((peers, slots + coarse_count, WIDTH), BF),
        grid=(1,),
        in_specs=[
            pl.BlockSpec(shape, lambda step: (0, 0))
            for shape in (leaf_multipoles.shape, (slots, peers), upward_ops.shape[::-1])
        ],
        out_specs=pl.BlockSpec((peers, slots + coarse_count, WIDTH), lambda step: (0, 0, 0)),
        scratch_shapes=[
            pltpu.VMEM((peers * slots, WIDTH), F32),
            pltpu.VMEM((8 * order_terms + 8, cell_count), F32),
        ],
        compiler_params=pltpu.CompilerParams(vmem_limit_bytes=60 << 20),
    )(leaf_multipoles, send_lists[0].T, upward_ops.T)
    arrived = lax.all_to_all(outgoing, "leaf", split_axis=0, concat_axis=0, tiled=True)

    local_cells = jnp.pad(leaf_multipoles, ((0, WIDTH - order_terms), (0, 0)))
    operators = arrange_classes(transfer_ops.T, order_terms)
    padded_classes = operators.shape[1] // WIDTH
    local_sum = pl.pallas_call(
        local_kernel,
        out_shape=jax.ShapeDtypeStruct((WIDTH, targets), F32),
        in_specs=[smem, vmem, vmem, vmem],
        out_specs=vmem,
        scratch_shapes=[
            pltpu.VMEM((padded_classes, targets), I32),
            pltpu.VMEM((WIDTH, cell_count), F32),
            pltpu.VMEM((GROUP * WIDTH, targets), BF),
        ],
        compiler_params=pltpu.CompilerParams(vmem_limit_bytes=24 << 20),
        cost_estimate=pl.CostEstimate(
            flops=0, bytes_accessed=30 * 1024 * 1024, transcendentals=0
        ),
    )(core.reshape(1), local_cells, leaf_pairs, operators)
    downward = arrange(downward_ops, order_terms)
    source_core = (top_pairs // coarse_count) % 2
    source_row = top_pairs // (2 * coarse_count) * coarse_count + top_pairs % coarse_count
    zero_row = peers * coarse_count
    held = (source_core == core) & (top_pairs < 2 * zero_row)
    coarse_pos = jnp.where(held, source_row, zero_row)
    coarse_pos = jnp.pad(
        coarse_pos, ((0, padded_classes - class_count), (0, 0)), constant_values=zero_row
    ).reshape(-1)

    most_tiles = (peers * slots + TILE - 1) // TILE
    half_shape = jax.ShapeDtypeStruct((WIDTH, cell_count), F32)
    keep, send = pl.pallas_call(
        functools.partial(main_kernel, order_terms),
        out_shape=(half_shape, half_shape),
        in_specs=[smem, smem] + [vmem] * 3 + [pl.BlockSpec(memory_space=pl.ANY), vmem],
        out_specs=(vmem, vmem),
        scratch_shapes=[
            pltpu.VMEM(operators.shape, BF),
            pltpu.SemaphoreType.DMA((FETCHES,)),
            pltpu.VMEM((padded_classes, targets), I32),
            pltpu.VMEM((most_tiles, 2 * WIDTH, HALF), BF),
            pltpu.VMEM((most_tiles, TILE // WIDTH, WIDTH, WIDTH), F32),
            pltpu.VMEM((zero_row + 8, WIDTH), F32),
            pltpu.VMEM((GROUP * coarse_targets, WIDTH), F32),
            pltpu.VMEM((GROUP * WIDTH, targets), BF),
            pltpu.VMEM((WIDTH, targets), F32),
            pltpu.VMEM((WIDTH, coarse_targets), F32),
        ],
        compiler_params=pltpu.CompilerParams(vmem_limit_bytes=51 << 20),
    )(core.reshape(1), coarse_pos, arrived, leaf_pairs, local_sum, operators, downward)
    other = lax.ppermute(send, "top", [(0, 1), (1, 0)])
    return (keep + other)[:order_terms]


def solution(mesh):
    in_specs = (
        P(None, ("leaf", "top")),
        P(),
        P(),
        P(),
        P(("leaf", "top"), None, None),
        P(None, "leaf"),
        P(None, "leaf"),
    )
    out_specs = P(None, ("leaf", "top"))
    return jax.shard_map(
        per_device, mesh=mesh, in_specs=in_specs, out_specs=out_specs, check_vma=False
    )
```

```python
import functools

import jax
import jax.numpy as jnp
from jax import lax
from jax.experimental import pallas as pl
from jax.experimental.pallas import tpu as pltpu
from jax.sharding import PartitionSpec as P

BF = jnp.bfloat16
F32 = jnp.float32
I32 = jnp.int32

WIDTH = 128
GROUP = 16
TILE = 384
HALF = 256
FETCHES = 4
SPAN = 8
COARSE_SPAN = 8
BY_PRODUCT = (0, 3, 6, 8, 11, 14)
BLOCK = 128


def nt_dot(left, right):
    return lax.dot_general(
        left, right, (((1,), (1,)), ((), ())), preferred_element_type=F32
    )


def dot(left, right):
    return jnp.dot(left, right, preferred_element_type=F32)


def main_kernel(
    flag_lane,
    core_ref,
    coarse_pos,
    arrived,
    pairs,
    local_sum,
    stored_operators,
    downward,
    keep,
    send,
    operators,
    arrivals,
    places,
    tables,
    columns,
    coarse_rows,
    picked,
    cells,
    near_sum,
    coarse_sum,
):
    piece = operators.shape[1] // FETCHES

    def fetch(index):
        span = pl.ds(pl.multiple_of(index * piece, WIDTH), piece)
        return pltpu.make_async_copy(
            stored_operators.at[:, span], operators.at[:, span], arrivals.at[index]
        )

    for index in range(FETCHES):
        fetch(index).start()
    core = core_ref[0]
    peers, rows_each, width = arrived.shape
    slots = rows_each // 2
    slot_count = peers * slots
    class_count, targets = pairs.shape
    groups = places.shape[0] // GROUP
    coarse_targets = coarse_sum.shape[1]
    local_count = targets // 2

    received = arrived[:, :slots, :].reshape(slot_count, width)
    flag_pick = (lax.broadcasted_iota(I32, (16, width), 1) == flag_lane).astype(F32).astype(BF)
    flags = nt_dot(flag_pick, received)
    by_peer = (
        lax.broadcasted_iota(I32, (slot_count, peers), 0) // slots
        == lax.broadcasted_iota(I32, (slot_count, peers), 1)
    )
    counts = dot(flags.astype(BF), by_peer.astype(F32).astype(BF))
    before = (
        lax.broadcasted_iota(I32, (peers, peers), 0) < lax.broadcasted_iota(I32, (peers, peers), 1)
    )
    first = dot(counts.astype(BF), before.astype(F32).astype(BF))[:8].astype(I32)
    used = jnp.sum(counts[0:1, :]).astype(I32)
    tile_count = (used + TILE - 1) // TILE

    lane = lax.broadcasted_iota(I32, (8, peers), 1)
    dest_parts = []
    for part in range(slots):
        slot = lane + part * peers
        at = jnp.take_along_axis(first, slot // slots, axis=1) + slot % slots
        live = flags[:8, part * peers : (part + 1) * peers] > 0.5
        dest_parts.append(jnp.where(live, at, -1))
    dest = jnp.concatenate(dest_parts, axis=1)[0:1]

    def place_rows(column):
        lines = column.shape[0]
        from_peer = jnp.broadcast_to(first[0:1], (lines, peers))
        parts = []
        for half in range(targets // peers):
            col = column[:, half * peers : (half + 1) * peers]
            slot = col - 2 * local_count - core * slot_count
            mine = (slot >= 0) & (slot < slot_count)
            safe = jnp.where(mine, slot, 0)
            far = jnp.take_along_axis(from_peer, safe // slots, axis=1) + safe % slots
            parts.append(jnp.where(mine, far, -1))
        return jnp.concatenate(parts, axis=1)

    lines = 32

    def place(block, _):
        start = pl.multiple_of(block * lines, lines)
        places[pl.ds(start, lines), :] = place_rows(pairs[pl.ds(start, lines), :])
        return 0

    whole = class_count // lines * lines
    lax.fori_loop(0, whole // lines, place, 0)
    for start in range(whole, class_count, 8):
        count = min(8, class_count - start)
        places[start : start + count, :] = place_rows(pairs[start : start + count, :])
    places[class_count:, :] = jnp.full((places.shape[0] - class_count, targets), -1, I32)

    def pack(tile, _):
        for part in range(TILE // peers):
            base = tile * TILE + part * peers
            one_hot = (
                lax.broadcasted_iota(I32, (peers, slot_count), 0) + base == dest
            ).astype(F32).astype(BF)
            packed = dot(one_hot, received).T.astype(BF)
            half, at = divmod(part * peers, HALF)
            tables[tile, half * width : (half + 1) * width, at : at + peers] = packed
            columns[tile, part] = packed.astype(F32)
        return 0

    tables[...] = jnp.zeros_like(tables)
    lax.fori_loop(0, jnp.maximum(tile_count, 1), pack, 0)

    coarse_rows[:slot_count, :] = arrived[:, slots:, :].reshape(slot_count, width).astype(F32)
    coarse_rows[slot_count:, :] = jnp.zeros((8, width), F32)

    near_sum[...] = local_sum[...]
    coarse_sum[...] = jnp.zeros_like(coarse_sum)
    row_index = lax.broadcasted_iota(I32, (HALF, targets), 0)

    def gather(table, position):
        inside = (position >= 0) & (position < TILE)
        low = jnp.where(inside, position & (HALF - 1), -1)
        one_hot = jnp.where(row_index == low, 1.0, 0.0).astype(BF)
        both = dot(table, one_hot)
        return jnp.where(position >= HALF, both[width:], both[:width]).astype(BF)

    def lane_gather(tile, position):
        blocks = []
        for half in range(targets // width):
            at = position[:, half * width : (half + 1) * width]
            lane_at = jnp.broadcast_to(at & (width - 1), (8, width))
            block = jnp.broadcast_to(at // width, (8, width))
            block = jnp.where(jnp.broadcast_to(at, (8, width)) < 0, -1, block)
            lines = []
            for line in range(0, width, 8):
                found = jnp.zeros((8, width), F32)
                for part in range(TILE // width):
                    picked_cells = jnp.take_along_axis(
                        columns[tile, part, line : line + 8, :], lane_at, axis=1
                    )
                    found = jnp.where(block == part, picked_cells, found)
                lines.append(found)
            blocks.append(jnp.concatenate(lines, axis=0))
        return jnp.concatenate(blocks, axis=1).astype(BF)

    def operator_span(group, done, count):
        start = pl.multiple_of((group * GROUP + done) * width, 2 * width)
        return operators[:, pl.ds(start, count * width)]

    def near_step(table, tile, group, base, gather_now=True):
        if gather_now:
            position = places[pl.ds(pl.multiple_of(group * GROUP, GROUP), GROUP), :] - base
        total = near_sum[...]
        for pair in range(GROUP // 2):
            here = slice(2 * pair * width, 2 * (pair + SPAN) * width)
            ready = jnp.maximum(group - 1, 0)
            if pair % SPAN == 0:
                total = total + dot(operator_span(ready, 2 * pair, 2 * SPAN), cells[here, :])
            if gather_now:
                for c in (2 * pair, 2 * pair + 1):
                    row = position[c : c + 1]
                    cells[c * width : (c + 1) * width, :] = (
                        gather(table, row) if c in BY_PRODUCT else lane_gather(tile, row)
                    )
        near_sum[...] = total

    def coarse_step(group, gather_now=True):
        total = coarse_sum[...]
        ready = jnp.maximum(group - 1, 0)
        base = group * (GROUP * coarse_targets)
        for done in range(0, GROUP, COARSE_SPAN):
            at = done * coarse_targets
            both = jnp.concatenate(
                [
                    picked[at + j * coarse_targets : at + (j + 1) * coarse_targets, :].astype(BF)
                    for j in range(COARSE_SPAN)
                ],
                axis=1,
            )
            total = total + nt_dot(operator_span(ready, done, COARSE_SPAN), both)
            if gather_now:
                for row in range(at, at + COARSE_SPAN * coarse_targets):
                    picked[pl.ds(row, 1), :] = coarse_rows[pl.ds(coarse_pos[base + row], 1), :]
        coarse_sum[...] = total

    picked[...] = jnp.zeros_like(picked)
    cells[...] = jnp.zeros_like(cells)

    def first_tile(group, _):
        near_step(tables[0], 0, group, 0)
        coarse_step(group)
        return 0

    steps = groups // FETCHES

    def fetched(index, _):
        fetch(index).wait()
        return lax.fori_loop(index * steps, (index + 1) * steps, first_tile, 0)

    lax.fori_loop(0, FETCHES, fetched, 0)
    coarse_step(groups, False)
    near_step(None, 0, groups, 0, False)

    def more_tiles(tile, _):
        table = tables[tile]
        cells[...] = jnp.zeros_like(cells)

        def step(group, _):
            near_step(table, tile, group, tile * TILE)
            return 0

        lax.fori_loop(0, groups, step, 0)
        near_step(None, tile, groups, 0, False)
        return 0

    lax.fori_loop(1, tile_count, more_tiles, 0)

    children = targets // coarse_targets
    spread = (
        lax.broadcasted_iota(I32, (coarse_targets, targets), 1) // children
        == lax.broadcasted_iota(I32, (coarse_targets, targets), 0)
    ).astype(F32).astype(BF)
    child = lax.broadcasted_iota(I32, (width, targets), 1) % children
    total = near_sum[...]
    real = lax.broadcasted_iota(I32, (width, coarse_targets), 0) < flag_lane
    rest = jnp.where(real, coarse_sum[...], 0.0)
    for _ in range(2):
        term = rest.astype(BF)
        rest = rest - term.astype(F32)
        wide = dot(term, spread)
        stacked = jnp.concatenate(
            [jnp.where(child == k, wide, 0.0).astype(BF) for k in range(children)], axis=0
        )
        total = total + dot(downward[...], stacked)
    left, right = total[:, :local_count], total[:, local_count:]
    keep[...] = jnp.where(core == 0, left, right)
    send[...] = jnp.where(core == 0, right, left)


def local_kernel(core_ref, local_cells, pairs, operators, local_sum, places, columns, cells):
    width, local_count = local_cells.shape
    class_count, targets = pairs.shape
    groups = places.shape[0] // GROUP
    first = core_ref[0] * local_count
    places[:class_count, :] = pairs[...] - first
    places[class_count:, :] = jnp.full((places.shape[0] - class_count, targets), -1, I32)
    columns[...] = local_cells[...].astype(F32)
    cells[...] = jnp.zeros_like(cells)
    local_sum[...] = jnp.zeros_like(local_sum)

    def translate(group):
        start = pl.multiple_of(group * GROUP * width, GROUP * width)
        local_sum[...] += dot(operators[:, pl.ds(start, GROUP * width)], cells[...])

    def step(group, _):
        translate(jnp.maximum(group - 1, 0))
        position = places[pl.ds(pl.multiple_of(group * GROUP, GROUP), GROUP), :]
        for c in range(GROUP):
            for half in range(targets // width):
                span = slice(half * width, (half + 1) * width)
                at = jnp.broadcast_to(position[c : c + 1, span], (8, width))
                live = (at >= 0) & (at < local_count)
                lane_at = at & (local_count - 1)
                lines = [
                    jnp.where(
                        live,
                        jnp.take_along_axis(columns[line : line + 8, :], lane_at, axis=1),
                        0.0,
                    )
                    for line in range(0, width, 8)
                ]
                cells[c * width : (c + 1) * width, span] = jnp.concatenate(lines, axis=0).astype(BF)
        return 0

    lax.fori_loop(0, groups, step, 0)
    translate(groups - 1)


def arrange(operators, order_terms):
    class_count = operators.shape[1] // order_terms
    arranged = operators.reshape(order_terms, class_count, order_terms).transpose(2, 1, 0)
    pad = WIDTH - order_terms
    arranged = jnp.pad(arranged, ((0, pad), (0, 0), (0, pad)))
    return arranged.reshape(WIDTH, class_count * WIDTH)


def arrange_kernel(class_count, source, arranged, rows):
    lines, order_terms = source.shape
    whole = rows.shape[0] - 8
    rows[:, order_terms:] = jnp.zeros((whole + 8, WIDTH - order_terms), F32)
    rows[whole:, :] = jnp.zeros((8, WIDTH), F32)
    for done in range(0, class_count, BLOCK):
        here = min(BLOCK, class_count - done)
        count = here * order_terms
        start = done * order_terms

        def widen(block, _):
            at = pl.multiple_of(block * WIDTH, WIDTH)
            rows[pl.ds(at, WIDTH), :order_terms] = source[pl.ds(start + at, WIDTH), :].astype(F32)
            return 0

        lax.fori_loop(0, count // WIDTH, widen, 0, unroll=4)
        left = count % WIDTH
        if left:
            rows[count - left : count, :order_terms] = source[
                start + count - left : start + count, :
            ].astype(F32)

        def cut(index, _):
            at = pl.multiple_of((done + index) * WIDTH, WIDTH)
            arranged[:, pl.ds(at, WIDTH)] = rows[pl.ds(index * order_terms, WIDTH), :].astype(BF)
            return 0

        lax.fori_loop(0, here, cut, 0, unroll=4)
    spare = arranged.shape[1] - class_count * WIDTH
    arranged[:, class_count * WIDTH :] = jnp.zeros((WIDTH, spare), BF)


def arrange_classes(operators, order_terms):
    class_count = operators.shape[0] // order_terms
    padded_count = (class_count + GROUP - 1) // GROUP * GROUP
    vmem = pl.BlockSpec(memory_space=pltpu.VMEM)
    return pl.pallas_call(
        functools.partial(arrange_kernel, class_count),
        out_shape=jax.ShapeDtypeStruct((WIDTH, padded_count * WIDTH), BF),
        in_specs=[vmem],
        out_specs=vmem,
        scratch_shapes=[pltpu.VMEM((BLOCK * order_terms + 8, WIDTH), F32)],
        compiler_params=pltpu.CompilerParams(vmem_limit_bytes=32 << 20),
        cost_estimate=pl.CostEstimate(
            flops=0, bytes_accessed=40 * 1024 * 1024, transcendentals=0
        ),
    )(operators)


def outgoing_kernel(cells, chosen, upward, outgoing, spread, risen):
    order_terms, cell_count = cells.shape
    slots, peers = chosen.shape
    coarse_count = cell_count // 8
    pad = WIDTH - order_terms
    values = cells[...].astype(F32)
    flag = (lax.broadcasted_iota(I32, (pad, cell_count), 0) == 0).astype(F32)
    flagged = jnp.concatenate([values, flag], axis=0).astype(BF)
    columns = jnp.concatenate(
        [chosen[...].astype(F32), jnp.zeros((peers - slots, peers), F32)], axis=0
    ).T.astype(I32)
    cell = lax.broadcasted_iota(I32, (peers, cell_count), 1)
    for slot in range(slots):
        one_hot = (cell == columns[:, slot : slot + 1]).astype(F32).astype(BF)
        spread[pl.ds(slot, peers, stride=slots), :] = nt_dot(one_hot, flagged)
    outgoing[:, :slots, :] = spread[...].astype(BF).reshape(peers, slots, WIDTH)

    risen[: 8 * order_terms, :] = dot(upward[...], cells[...])
    risen[8 * order_terms :, :] = jnp.zeros((8, cell_count), F32)
    child = lax.broadcasted_iota(I32, (WIDTH, cell_count), 1) % 8
    total = jnp.zeros((WIDTH, cell_count), F32)
    for k in range(8):
        total = total + jnp.where(child == k, risen[pl.ds(k * order_terms, WIDTH), :], 0.0)
    real = lax.broadcasted_iota(I32, (WIDTH, cell_count), 0) < order_terms
    total = jnp.where(real, total, 0.0).T
    coarse = jnp.sum(total.reshape(coarse_count, 8, WIDTH), axis=1).astype(BF)
    outgoing[:, slots:, :] = jnp.broadcast_to(coarse[None], (peers, coarse_count, WIDTH))


def per_device(
    leaf_multipoles, upward_ops, transfer_ops, downward_ops, send_lists, leaf_pairs, top_pairs
):
    order_terms, cell_count = leaf_multipoles.shape
    _, peers, slots = send_lists.shape
    class_count, targets = leaf_pairs.shape
    coarse_targets = top_pairs.shape[1]
    coarse_count = cell_count // 8
    core = lax.axis_index("top").astype(I32)
    vmem = pl.BlockSpec(memory_space=pltpu.VMEM)
    smem = pl.BlockSpec(memory_space=pltpu.SMEM)

    outgoing = pl.pallas_call(
        outgoing_kernel,
        out_shape=jax.ShapeDtypeStruct((peers, slots + coarse_count, WIDTH), BF),
        grid=(1,),
        in_specs=[
            pl.BlockSpec(shape, lambda step: (0, 0))
            for shape in (leaf_multipoles.shape, (slots, peers), upward_ops.shape[::-1])
        ],
        out_specs=pl.BlockSpec((peers, slots + coarse_count, WIDTH), lambda step: (0, 0, 0)),
        scratch_shapes=[
            pltpu.VMEM((peers * slots, WIDTH), F32),
            pltpu.VMEM((8 * order_terms + 8, cell_count), F32),
        ],
        compiler_params=pltpu.CompilerParams(vmem_limit_bytes=60 << 20),
    )(leaf_multipoles, send_lists[0].T, upward_ops.T)
    arrived = lax.all_to_all(outgoing, "leaf", split_axis=0, concat_axis=0, tiled=True)

    local_cells = jnp.pad(leaf_multipoles, ((0, WIDTH - order_terms), (0, 0)))
    operators = arrange_classes(transfer_ops.T, order_terms)
    padded_classes = operators.shape[1] // WIDTH
    local_sum = pl.pallas_call(
        local_kernel,
        out_shape=jax.ShapeDtypeStruct((WIDTH, targets), F32),
        in_specs=[smem, vmem, vmem, vmem],
        out_specs=vmem,
        scratch_shapes=[
            pltpu.VMEM((padded_classes, targets), I32),
            pltpu.VMEM((WIDTH, cell_count), F32),
            pltpu.VMEM((GROUP * WIDTH, targets), BF),
        ],
        compiler_params=pltpu.CompilerParams(vmem_limit_bytes=24 << 20),
        cost_estimate=pl.CostEstimate(
            flops=0, bytes_accessed=30 * 1024 * 1024, transcendentals=0
        ),
    )(core.reshape(1), local_cells, leaf_pairs, operators)
    downward = arrange(downward_ops, order_terms)
    source_core = (top_pairs // coarse_count) % 2
    source_row = top_pairs // (2 * coarse_count) * coarse_count + top_pairs % coarse_count
    zero_row = peers * coarse_count
    held = (source_core == core) & (top_pairs < 2 * zero_row)
    coarse_pos = jnp.where(held, source_row, zero_row)
    coarse_pos = jnp.pad(
        coarse_pos, ((0, padded_classes - class_count), (0, 0)), constant_values=zero_row
    ).reshape(-1)

    most_tiles = (peers * slots + TILE - 1) // TILE
    half_shape = jax.ShapeDtypeStruct((WIDTH, cell_count), F32)
    keep, send = pl.pallas_call(
        functools.partial(main_kernel, order_terms),
        out_shape=(half_shape, half_shape),
        in_specs=[smem, smem] + [vmem] * 3 + [pl.BlockSpec(memory_space=pl.ANY), vmem],
        out_specs=(vmem, vmem),
        scratch_shapes=[
            pltpu.VMEM(operators.shape, BF),
            pltpu.SemaphoreType.DMA((FETCHES,)),
            pltpu.VMEM((padded_classes, targets), I32),
            pltpu.VMEM((most_tiles, 2 * WIDTH, HALF), BF),
            pltpu.VMEM((most_tiles, TILE // WIDTH, WIDTH, WIDTH), F32),
            pltpu.VMEM((zero_row + 8, WIDTH), F32),
            pltpu.VMEM((GROUP * coarse_targets, WIDTH), F32),
            pltpu.VMEM((GROUP * WIDTH, targets), BF),
            pltpu.VMEM((WIDTH, targets), F32),
            pltpu.VMEM((WIDTH, coarse_targets), F32),
        ],
        compiler_params=pltpu.CompilerParams(vmem_limit_bytes=51 << 20),
    )(core.reshape(1), coarse_pos, arrived, leaf_pairs, local_sum, operators, downward)
    other = lax.ppermute(send, "top", [(0, 1), (1, 0)])
    return (keep + other)[:order_terms]


def solution(mesh):
    in_specs = (
        P(None, ("leaf", "top")),
        P(),
        P(),
        P(),
        P(("leaf", "top"), None, None),
        P(None, "leaf"),
        P(None, "leaf"),
    )
    out_specs = P(None, ("leaf", "top"))
    return jax.shard_map(
        per_device, mesh=mesh, in_specs=in_specs, out_specs=out_specs, check_vma=False
    )
```
